128 devices in a mesh: replica: 8 (over y_hi, z), tensor: 16 (over x, y_lo, core).
Axes of the slice: x: 4, y: 4 (y_hi: 2, y_lo: 2; y = y_hi * 2 + y_lo), z: 4, core: 2. Of those that a mesh axis runs over, the one named last changes fastest.
Arguments:
- features: bfloat16 [1536, 3, 8192], P('replica', None, 'tensor'), may hold values from -6 to 6
- accepted: int32 [8], P('replica'), may hold values from 96 to 192
- owner: int32 [1536, 1], P('replica'), may hold values from 0 to 15; in each aligned block of 1536 rows (0 to 1535, 1536 to 3071, ...) at most 192 rows name the same one
- draft_ids: int32 [1536], P('replica'), may hold values from 0 to 31999
- fc_weight: bfloat16 [3, 8192, 8192], P(None, 'tensor', 'replica'), may hold values from -0.0390625 to 0.0390625
- embed_table: bfloat16 [32000, 8192], P('tensor', 'replica'), may hold values from -6 to 6
- embed_gain: float32 [8192], P('replica'), may hold values from 0.1 to 1.9
- hidden_gain: float32 [8192], P('replica'), may hold values from 0.1 to 1.9
- hidden_grad: bfloat16 [3072, 8192], P('tensor', 'replica'), may hold values from -6 to 6
Outputs:
- draft_input: bfloat16 [3072, 2, 8192], P('tensor', None, 'replica')
- grad_fc: float32 [3, 8192, 8192], P(None, 'tensor', 'replica')
The draws below stay inside these ranges and needn't reach their ends.
Inputs may be any that keep to these rules, and one draw needn't show every extreme that they name: Over all 1536 rows no owner is named by more than 192 rows, a bound that some block reaches.
All inputs are finite; a program needn't handle non-finite values.
Results may differ from the reference program's by a relative error of at most 0.0029.
Values may be sent and summed in bfloat16 or wider, within the bound.
No kernel may reach another device: no remote copies, remote signals or barrier semaphores. Data moves between devices by JAX's collectives and lax.ppermute only.
A program may use at most 128 MiB of HBM per device.

```python
import math
import jax
import jax.numpy as jnp
import numpy as np
from jax import lax

D = 8192
VOCAB = 32000
TAPS = 3
SRV = 192
ROWS = 1536
CAP = 192
SLOTS = 3072
N_REPLICA = 8
N_TENSOR = 16


def plant(drawn, own_key, low, high):
    longest = drawn.shape.index(max(drawn.shape))
    spots = []
    for shift in (0, 1):
        where = [jax.random.randint(jax.random.fold_in(own_key, axis), (), 0, length) for axis, length in enumerate(drawn.shape)]
        where[longest] = (where[longest] + shift) % drawn.shape[longest]
        spots.append(tuple(where))
    return drawn.at[spots[0]].set(low).at[spots[1]].set(high)


def steps_of(key, extent, cuts, least, largest):
    def one(position, parts):
        draws = jax.random.uniform(jax.random.fold_in(jax.random.fold_in(key, 6), position), (parts,), jnp.float32, least / len(cuts), largest / len(cuts))
        return jnp.repeat(jnp.exp(draws), extent[position] // parts).reshape((-1,) + (1,) * (len(extent) - position - 1))

    level = one(*cuts[0])
    for cut in cuts[1:]:
        level = level * one(*cut)
    return level


def cumulative_ranks(amount, slope):
    loads = [(1 << 20) // math.isqrt(grade ** slope) + 1 for grade in range(1, amount + 1)]
    spread = 1 + sum(loads) // (1 << 30)
    return np.cumsum(np.array([max(1, weight // spread) for weight in loads]))


def skewed_ids(key, dims, amount, lean):
    grid = cumulative_ranks(amount, lean)
    lot = jax.random.randint(jax.random.fold_in(key, 1), dims, 0, int(grid[amount - 1]))
    standing = jnp.searchsorted(jnp.asarray(grid, jnp.int32), lot, side="right")
    return jax.random.permutation(jax.random.fold_in(key, 2), amount)[standing].astype(jnp.int32)


def shared_out(key, own, number, rows, number_of, top, most, skew):
    order = jax.random.permutation(key, number_of)
    heavy_load, ordinary = shares(number_of, rows * top, most, skew, True), shares(number_of, rows * top, most, skew, False)
    places = jnp.arange(number_of)

    def named(tallies, offset_by):
        used = int((tallies > 0).sum())
        fixed = max(1, used // 4)
        moved = fixed + (places - fixed + offset_by * (used - fixed)) % max(1, number_of - fixed)
        return jnp.zeros((number_of,), jnp.int32).at[order[jnp.where(places < fixed, places, moved)]].set(jnp.asarray(tallies, jnp.int32))

    tallies = jnp.where(number % 4 == 0, named(heavy_load, number // 4), named(ordinary, number - number // 4 - 1))
    mixed = jax.random.permutation(jax.random.fold_in(own, 3), number_of)
    source_of, taker = mixed[0:number_of // 2 * 2:2], mixed[1:number_of // 2 * 2:2]
    margin = jnp.minimum(tallies[source_of] - 1, most - tallies[taker]) // 2
    margin = jnp.where((source_of == order[0]) | (taker == order[0]) | (tallies[taker] == 0), 0, jnp.maximum(margin, 0))
    moved = jax.random.randint(jax.random.fold_in(own, 4), (number_of // 2,), 0, 1 << 20) % (margin + 1)
    tallies = tallies.at[source_of].add(-moved).at[taker].add(moved)
    members = jnp.searchsorted(jnp.cumsum(tallies), jnp.arange(rows * top), side="right").astype(jnp.int32)
    grid = members.reshape(top, rows).T
    grid = grid[jax.random.permutation(jax.random.fold_in(own, 1), rows)]
    offset_by = jax.random.randint(jax.random.fold_in(own, 2), (rows, 1), 0, top)
    return jnp.take_along_axis(grid, (jnp.arange(top)[None, :] + offset_by) % top, axis=1)


def shares(amount, total, most, slope, full):
    weights = [(1 << 20) // math.isqrt(standing ** slope) + 1 for standing in range(1, amount + 1)]
    largest = most if full else min(most, max(-(-total // amount), total * weights[0] // sum(weights)))
    least = 1 if total - largest >= amount - 1 else 0
    given, rest = [largest] + [least] * (amount - 1), total - largest - least * (amount - 1)
    while rest > 0:
        free = [i for i in range(1, amount) if given[i] < largest] or [i for i in range(1, amount) if given[i] < most]
        mass, budget = sum([weights[i] for i in free]), rest
        for i in free:
            extra = min(most - given[i], max(1, budget * weights[i] // mass), rest)
            given[i] = given[i] + extra
            rest = rest - extra
    return np.array(given)


def bell_draw(rng, extent, scale, bound, pieces=(), kind=jnp.bfloat16):
    entries = scale * jax.random.normal(rng, extent, jnp.float32)
    if pieces:
        entries = entries * steps_of(rng, extent, pieces, -0.22, 0.18)
    return jnp.clip(entries, -bound, bound).astype(kind)


def setup_inputs(seed: int = 0) -> dict:
    streams_of = jax.random.split(jax.random.key(seed), 10)
    features = bell_draw(streams_of[0], (ROWS, TAPS, D), 1.0, 6.0, ((0, 8), (2, 16)))
    accepted = plant(jax.random.randint(streams_of[1], (N_REPLICA,), SRV // 2, SRV + 1), jax.random.fold_in(streams_of[1], 1), SRV // 2, SRV).astype(jnp.int32)
    owner_keys = jax.random.split(jax.random.fold_in(streams_of[2], 1), ROWS // ROWS)
    owner_turns = jax.random.permutation(jax.random.fold_in(streams_of[2], 3), ROWS // ROWS)
    owner = jax.vmap(lambda own, number: shared_out(jax.random.fold_in(streams_of[2], 2), own, number, ROWS, N_TENSOR, 1, CAP, 2))(owner_keys, owner_turns).reshape((ROWS, 1))
    draft_ids = plant(skewed_ids(streams_of[3], (ROWS,), VOCAB, 2), jax.random.fold_in(streams_of[3], 3), 0, VOCAB - 1).astype(jnp.int32)
    fc_weight = bell_draw(streams_of[4], (TAPS, D, D), (TAPS * D) ** -0.5, 0.0390625, ((1, 16), (2, 8)))
    embed_table = bell_draw(streams_of[5], (VOCAB, D), 1.0, 6.0, ((0, 16), (1, 8)))
    embed_gain = jnp.clip(1.0 + 0.18 * jax.random.normal(streams_of[6], (D,), jnp.float32), 0.1, 1.9)
    hidden_gain = jnp.clip(1.0 + 0.18 * jax.random.normal(streams_of[7], (D,), jnp.float32), 0.1, 1.9)
    hidden_grad = bell_draw(streams_of[8], (SLOTS, D), 1.0, 6.0, ((0, 16), (1, 8)))
    return dict(features=features, accepted=accepted, owner=owner, draft_ids=draft_ids, fc_weight=fc_weight, embed_table=embed_table, embed_gain=embed_gain, hidden_gain=hidden_gain, hidden_grad=hidden_grad)


EPSILON = 1e-05

def slot_layout(accepted, owners, per_server, capacity, owner_count):
    row_total = owners.shape[0]
    row_index = jnp.arange(row_total, dtype=jnp.int32)
    limits = jnp.repeat(accepted, per_server, total_repeat_length=row_total)
    valid = row_index % per_server < limits
    picks = ((owners[:, None] == jnp.arange(owner_count, dtype=jnp.int32)[None, :]) & valid[:, None]).astype(jnp.int32)
    before = jnp.cumsum(picks, axis=0) - picks
    ranking = lax.optimization_barrier(jnp.sum(before * picks, axis=1))
    slot_total = owner_count * capacity
    target = jnp.where(valid, owners * capacity + ranking, slot_total).astype(jnp.int32)
    source = jnp.zeros((slot_total,), jnp.int32).at[target].set(row_index, mode='drop')
    filled = jnp.zeros((slot_total,), jnp.int32).at[target].set(1, mode='drop')
    return (valid, target, source, filled)

def reference(features, accepted, owner, draft_ids, fc_weight, embed_table, embed_gain, hidden_gain, hidden_grad):
    row_total = features.shape[0]
    valid, target, source, filled = slot_layout(accepted, owner[:, 0], SRV, CAP, N_TENSOR)
    row_feats = features.reshape(row_total, TAPS * D)
    united_rows = jnp.dot(row_feats, fc_weight.reshape(TAPS * D, D), preferred_element_type=jnp.float32)
    present = (filled > 0)[:, None]
    united = jnp.where(present, united_rows[source], jnp.float32(0.0))
    embeds = jnp.where(present, embed_table[draft_ids[source]].astype(jnp.float32), jnp.float32(0.0))
    r_hidden = lax.rsqrt(lax.optimization_barrier(jnp.mean(united * united, axis=-1, keepdims=True)) + EPSILON)
    r_embed = lax.rsqrt(lax.optimization_barrier(jnp.mean(embeds * embeds, axis=-1, keepdims=True)) + EPSILON)
    draft_input = jnp.stack([embeds * r_embed * embed_gain, united * r_hidden * hidden_gain], axis=1).astype(jnp.bfloat16)
    weighted = jnp.where(present, hidden_grad.astype(jnp.float32) * hidden_gain, jnp.float32(0.0))
    inner = lax.optimization_barrier(jnp.sum(united * weighted, axis=-1, keepdims=True))
    united_grad = (r_hidden * weighted - r_hidden ** 3 * united * inner / D).astype(jnp.bfloat16)
    picked = jnp.minimum(target, CAP * N_TENSOR - 1)
    row_grad = jnp.where(valid[:, None], united_grad[picked], jnp.zeros((), jnp.bfloat16))
    grad_fc = jnp.dot(row_feats.T, row_grad, preferred_element_type=jnp.float32).reshape(TAPS, D, D)
    return (draft_input, grad_fc)
```

```python
import functools

import jax
import jax.numpy as jnp
from jax import lax
from jax.experimental import pallas as pl
from jax.experimental.pallas import tpu as pltpu
from jax.sharding import PartitionSpec as P

TAPS = 3
EPSILON = 1e-05
BF = jnp.bfloat16
F32 = jnp.float32
I32 = jnp.int32
SPREAD = 112
CHUNK = 48
RIDE = 32
LONG = pl.CostEstimate(flops=10**11, bytes_accessed=10**9, transcendentals=0)
SHORT = pl.CostEstimate(flops=10**6, bytes_accessed=10**5, transcendentals=0)
MIB = 1024 * 1024
OWNERS = 16
REPLICAS = 8

CHIP_GROUPS = [[2 * chip + core for chip in range(8)] for core in (0, 1)]
CORE_SWAP = [(i, i ^ 1) for i in range(16)]
Y_SWAP = [(i, i ^ 4) for i in range(8)]
Z_UP = [(i, i // 4 * 4 + (i + 1) % 4) for i in range(8)]
Z_DOWN = [(i, i // 4 * 4 + (i + 3) % 4) for i in range(8)]


def to_chips(x):
    return lax.all_to_all(x, "tensor", 0, 0, axis_index_groups=CHIP_GROUPS)


def from_replicas(x):
    spread = jnp.broadcast_to(x[None], (REPLICAS,) + x.shape)
    return lax.all_to_all(spread, "replica", 0, 0)


def swap_cores(x):
    return lax.ppermute(x, "tensor", CORE_SWAP)


def dot(a, b):
    return jnp.dot(a, b, preferred_element_type=F32)


def together(*xs):
    return lax.optimization_barrier(xs)


def pick(x, index, axis=0):
    return lax.dynamic_index_in_dim(x, index, axis, keepdims=False)


def whole(shape):
    return pl.BlockSpec(shape, lambda *_: (0,) * len(shape))


def project(sides, weight, which, out_dtype, cost):
    per_server, cols = sides[0][0].shape[1], weight.shape[1]
    first = len(sides[0])
    total = first + len(sides[1])

    def kernel(which_ref, *refs):
        w_ref, out_ref = refs[total:]

        def run(pieces):
            x = jnp.concatenate(
                [jnp.concatenate([p[t] for p in pieces], axis=0) for t in range(TAPS)], axis=1
            )
            out_ref[...] = dot(x, w_ref[...]).astype(out_ref.dtype)

        @pl.when(which_ref[0] == 0)
        def _():
            run(refs[:first])

        @pl.when(which_ref[0] != 0)
        def _():
            run(refs[first:total])

    vmem = pl.BlockSpec()
    return pl.pallas_call(
        kernel,
        out_shape=jax.ShapeDtypeStruct((2 * per_server, cols), out_dtype),
        in_specs=[pl.BlockSpec(memory_space=pltpu.SMEM)] + [vmem] * (total + 1),
        out_specs=vmem,
        compiler_params=pltpu.CompilerParams(vmem_limit_bytes=24 * 1024 * 1024),
        cost_estimate=cost,
        name="project",
    )(which.reshape(1), *sides[0], *sides[1], weight)


def sum_and_spread(parts, extra):
    chips, each, cols = parts.shape
    more = extra.shape[1]

    def kernel(parts_ref, extra_ref, out_ref):
        out_ref[:, each : each + more] = extra_ref[...]
        for first in range(0, each, 16):
            here = slice(first, first + 16)
            total = parts_ref[0, here].astype(F32)
            for k in range(1, chips):
                total = total + parts_ref[k, here].astype(F32)
            total = total.astype(BF)
            for k in range(chips):
                out_ref[k, here] = total

    vmem = pl.BlockSpec()
    return pl.pallas_call(
        kernel,
        out_shape=jax.ShapeDtypeStruct((chips, each + more, cols), BF),
        in_specs=[vmem] * 2,
        out_specs=vmem,
        compiler_params=pltpu.CompilerParams(vmem_limit_bytes=16 * MIB),
        cost_estimate=SHORT,
        name="sum_and_spread",
    )(parts, extra)


def take_rows(position, value, tables, count, step):
    length, cols = tables[0].shape
    total = position.shape[1]

    def kernel(position_ref, value_ref, *refs):
        first = pl.program_id(0) * step
        row = lax.broadcasted_iota(I32, (step, total), 0) + first
        match = row == position_ref[...]
        index = jnp.sum(jnp.where(match, value_ref[...] + 1, 0), axis=1, keepdims=True) - 1
        found = None
        for at, table_ref in enumerate(refs[:-1]):
            hot = lax.broadcasted_iota(I32, (step, length), 1) + at * length == index
            part = dot(jnp.where(hot, 1.0, 0.0).astype(BF), table_ref[...])
            found = part if found is None else found + part
        refs[-1][...] = found.astype(BF)

    return pl.pallas_call(
        kernel,
        grid=(count // step,),
        out_shape=jax.ShapeDtypeStruct((count, cols), BF),
        in_specs=[whole((1, total)), whole((1, total))] + [whole((length, cols))] * len(tables),
        out_specs=pl.BlockSpec((step, cols), lambda i: (i, 0)),
        compiler_params=pltpu.CompilerParams(vmem_limit_bytes=40 * MIB),
        cost_estimate=LONG,
        name="take_rows",
    )(position, value, *tables)


def add_halves(keeps, received):
    pair, cols = keeps[0].shape
    each = pair // 8

    def kernel(k0, r0, k1, r1, out_ref):
        for chip in range(8):
            rows = slice(chip * each, chip * each + each)
            for at, (k, r) in enumerate(((k0, r0), (k1, r1))):
                total = (k[rows] + r[rows].astype(F32)).astype(BF)
                out_ref[chip, at * each : at * each + each] = total

    vmem = pl.BlockSpec()
    return pl.pallas_call(
        kernel,
        out_shape=jax.ShapeDtypeStruct((8, 2 * each, cols), BF),
        in_specs=[vmem] * 4,
        out_specs=vmem,
        compiler_params=pltpu.CompilerParams(vmem_limit_bytes=16 * MIB),
        cost_estimate=SHORT,
        name="add_halves",
    )(keeps[0], received[0], keeps[1], received[1])


def add_split(a, b, parts):
    size = a.shape[0] // parts
    cols = a.shape[1]

    def kernel(a_ref, b_ref, *outs):
        for k, out in enumerate(outs):
            out[...] = a_ref[k * size : k * size + size] + b_ref[k * size : k * size + size]

    vmem = pl.BlockSpec()
    return pl.pallas_call(
        kernel,
        out_shape=[jax.ShapeDtypeStruct((size, cols), BF)] * parts,
        in_specs=[vmem] * 2,
        out_specs=[vmem] * parts,
        compiler_params=pltpu.CompilerParams(vmem_limit_bytes=16 * MIB),
        cost_estimate=SHORT,
        name="add_split",
    )(a, b)


def rows_at(united_refs, place):
    ref = united_refs[place // 4]
    size = CHUNK
    chunk = place % 4 // 2
    block = ref[4 * (place % 2) : 4 * (place % 2) + 4, chunk * size : chunk * size + size]
    return block.reshape(4 * size, ref.shape[2])


def landed_rows(own_ref):
    block = own_ref[:, 2 * CHUNK : 2 * CHUNK + RIDE].astype(F32)[:, :24]
    return block.reshape(8 * 24, block.shape[2])


def column_of(row, size):
    eye = lax.broadcasted_iota(I32, (size, size), 0) == lax.broadcasted_iota(I32, (size, size), 1)
    return jnp.sum(jnp.where(eye, row, 0.0), axis=1, keepdims=True)


def row_of(column, size):
    eye = lax.broadcasted_iota(I32, (size, size), 0) == lax.broadcasted_iota(I32, (size, size), 1)
    return jnp.sum(jnp.where(eye, column, 0.0), axis=0, keepdims=True)


def half_sums(rows, cots, gain, per_server):
    cols = gain.shape[1]
    side = 4 * per_server

    def kernel(rows_ref, cots_ref, gain_ref, out_ref):
        for k in range(4):
            u = rows_at((rows_ref,), k).astype(F32)
            w = cots_ref[k * per_server : k * per_server + per_server].astype(F32) * gain_ref[...]
            square = row_of(jnp.sum(u * u, axis=1, keepdims=True), per_server)
            inner = row_of(jnp.sum(u * w, axis=1, keepdims=True), per_server)
            out_ref[k] = jnp.concatenate([square, inner], axis=0)

    return pl.pallas_call(
        kernel,
        grid=(1,),
        out_shape=jax.ShapeDtypeStruct((4, 2, per_server), F32),
        in_specs=[
            whole(rows.shape),
            pl.BlockSpec((side, cols), lambda i: (0, 0)),
            whole((1, cols)),
        ],
        out_specs=whole((4, 2, per_server)),
        compiler_params=pltpu.CompilerParams(vmem_limit_bytes=24 * MIB),
        cost_estimate=SHORT,
        name="half_sums",
    )(rows, cots, gain)


def partial_sums(order, sums, own, other, cots, gain, per_server):
    cols = gain.shape[1]
    side = 4 * per_server

    def kernel(order_ref, sums_ref, own_ref, other_ref, cots_ref, gain_ref, out_ref):
        for k in range(4):
            u = rows_at((other_ref,), k).astype(F32)
            w = cots_ref[k * per_server : k * per_server + per_server].astype(F32) * gain_ref[...]
            square = row_of(jnp.sum(u * u, axis=1, keepdims=True), per_server)
            inner = row_of(jnp.sum(u * w, axis=1, keepdims=True), per_server)
            both = jnp.concatenate([square, inner], axis=0)
            for to in range(REPLICAS):
                out_ref[to, order_ref[k]] = sums_ref[k]
                out_ref[to, order_ref[k + 4]] = both
        e = landed_rows(own_ref).astype(F32)
        square = row_of(jnp.sum(e * e, axis=1, keepdims=True), per_server)
        both = jnp.concatenate([square, square], axis=0)
        for to in range(REPLICAS):
            out_ref[to, REPLICAS] = both

    shape = (REPLICAS, REPLICAS + 1, 2, per_server)
    return pl.pallas_call(
        kernel,
        grid=(1,),
        out_shape=jax.ShapeDtypeStruct(shape, F32),
        in_specs=[
            pl.BlockSpec(memory_space=pltpu.SMEM),
            whole(sums.shape),
            whole(own.shape),
            whole(other.shape),
            pl.BlockSpec((side, cols), lambda i: (1, 0)),
            whole((1, cols)),
        ],
        out_specs=whole(shape),
        compiler_params=pltpu.CompilerParams(vmem_limit_bytes=24 * MIB),
        cost_estimate=SHORT,
        name="partial_sums",
    )(order, sums, own, other, cots, gain)


def turn(pieces):
    taps, _, feat = pieces[0].shape
    rows = sum(piece.shape[1] for piece in pieces)

    def kernel(*refs):
        x = jnp.concatenate([ref[0] for ref in refs[:-1]], axis=0)
        refs[-1][0] = x.T

    return pl.pallas_call(
        kernel,
        grid=(taps,),
        out_shape=jax.ShapeDtypeStruct((taps, feat, rows), BF),
        in_specs=[pl.BlockSpec((1, p.shape[1], feat), lambda t: (t, 0, 0)) for p in pieces],
        out_specs=pl.BlockSpec((1, feat, rows), lambda t: (t, 0, 0)),
        compiler_params=pltpu.CompilerParams(vmem_limit_bytes=24 * MIB),
        cost_estimate=SHORT,
        name="turn",
    )(*pieces)


def weight_gradient(order, core, turned, united, cots, gain, totals, model):
    taps, feat, rows = turned.shape
    per_server = rows // REPLICAS
    cols = cots.shape[1]
    places = ([0, 1, 4, 5, 2, 3, 6, 7], [4, 5, 0, 1, 6, 7, 2, 3])

    def kernel(order_ref, core_ref, *refs):
        united_refs = refs[1:3]
        turned_ref, cots_ref, gain_ref, totals_ref, out_ref, g_ref = refs[:1] + refs[3:]

        @pl.when(pl.program_id(0) == 0)
        def _():
            for place in range(REPLICAS):
                both = totals_ref[0, order_ref[place]]
                for source in range(1, REPLICAS):
                    both = both + totals_ref[source, order_ref[place]]
                r = lax.rsqrt(both[0:1] / model + EPSILON)
                s = r * r * both[1:2] / model
                r = column_of(r, per_server)
                s = column_of(s, per_server)
                here = jnp.where(core_ref[0] == 0, places[0].index(place), places[1].index(place))
                size = per_server // 4
                for part in range(4):
                    at = part * size
                    chunk = place % 4 // 2 * size
                    u = united_refs[place // 4][4 * (place % 2) + part, chunk : chunk + size]
                    u = u.astype(F32)
                    w = cots_ref[place * per_server + at : place * per_server + at + size]
                    w = w.astype(F32) * gain_ref[...]
                    g = r[at : at + size] * (w - u * s[at : at + size])
                    start = pl.multiple_of(here * per_server + at, size)
                    g_ref[pl.ds(start, size)] = g.astype(BF)

        out_ref[0] = dot(turned_ref[0], g_ref[...])

    smem = pl.BlockSpec(memory_space=pltpu.SMEM)
    return pl.pallas_call(
        kernel,
        grid=(taps,),
        out_shape=jax.ShapeDtypeStruct((taps, feat, cols), F32),
        in_specs=[smem, smem]
        + [pl.BlockSpec((1, feat, rows), lambda t: (t, 0, 0))]
        + [whole(united[0].shape)] * 2
        + [whole((rows, cols)), whole((1, cols)), whole(totals.shape)],
        out_specs=pl.BlockSpec((1, feat, cols), lambda t: (t, 0, 0)),
        scratch_shapes=[pltpu.VMEM((rows, cols), BF)],
        compiler_params=pltpu.CompilerParams(vmem_limit_bytes=48 * MIB),
        cost_estimate=LONG,
        name="weight_gradient",
    )(order, core.reshape(1), turned, *united, cots, gain, totals)


def slot_rows(order, position, united, capacity):
    cols = united[0].shape[2]
    per_server = position.shape[2]

    def kernel(order_ref, position_ref, own_ref, other_ref, out_ref):
        slot = lax.broadcasted_iota(I32, (capacity, per_server), 0)
        found = jnp.zeros((capacity, cols), F32)
        for place in range(REPLICAS):
            match = slot == position_ref[order_ref[place]]
            hot = jnp.where(match, 1.0, 0.0).astype(BF)
            found = found + dot(hot, rows_at((own_ref, other_ref), place))
        out_ref[...] = found.astype(BF)

    vmem = pl.BlockSpec()
    return pl.pallas_call(
        kernel,
        out_shape=jax.ShapeDtypeStruct((capacity, cols), BF),
        in_specs=[pl.BlockSpec(memory_space=pltpu.SMEM)] + [vmem] * 3,
        out_specs=vmem,
        compiler_params=pltpu.CompilerParams(vmem_limit_bytes=24 * MIB),
        cost_estimate=SHORT,
        name="slot_rows",
    )(order, position, *united)


def normed_rows(position, found, own, gain, embed_gain, totals, model):
    capacity, cols = found.shape
    per_server = position.shape[2]

    def kernel(
        position_ref, found_ref, own_ref, gain_ref, embed_gain_ref, totals_ref, embed_ref, out_ref
    ):
        slot = lax.broadcasted_iota(I32, (capacity, per_server), 0)
        r_slot = jnp.zeros((capacity, 1), F32)
        for replica in range(REPLICAS + 1):
            square = totals_ref[0, replica]
            for source in range(1, REPLICAS):
                square = square + totals_ref[source, replica]
            r = lax.rsqrt(square[0:1] / model + EPSILON)
            if replica < REPLICAS:
                match = slot == position_ref[replica]
                r_slot = r_slot + jnp.sum(jnp.where(match, r, 0.0), axis=1, keepdims=True)
            else:
                r_embed = column_of(r, per_server)
        out_ref[...] = (found_ref[...].astype(F32) * r_slot * gain_ref[...]).astype(BF)
        embed_ref[...] = (landed_rows(own_ref) * r_embed * embed_gain_ref[...]).astype(BF)

    vmem = pl.BlockSpec()
    return pl.pallas_call(
        kernel,
        out_shape=[jax.ShapeDtypeStruct((capacity, cols), BF)] * 2,
        in_specs=[vmem] * 6,
        out_specs=[vmem] * 2,
        compiler_params=pltpu.CompilerParams(vmem_limit_bytes=16 * MIB),
        cost_estimate=SHORT,
        name="normed_rows",
    )(position, found, own, gain, embed_gain, totals)


def body(
    features,
    accepted,
    owner,
    draft_ids,
    fc_weight,
    embed_table,
    embed_gain,
    hidden_gain,
    hidden_grad,
):
    tensor_index = lax.axis_index("tensor")
    replica_index = lax.axis_index("replica")
    core = tensor_index % 2
    y_hi = replica_index // 4
    z = replica_index % 4
    per_server = features.shape[0]
    capacity = hidden_grad.shape[0]
    steps = capacity // OWNERS
    feat = features.shape[2]
    width = TAPS * feat
    cols = fc_weight.shape[2]
    model = cols * REPLICAS
    rows = per_server * REPLICAS
    pair = 2 * per_server

    weight = fc_weight.reshape(width, cols)

    with jax.named_scope("gather_cotangents"):
        grads = lax.all_gather(hidden_grad, "tensor", axis=0, tiled=True)

    with jax.named_scope("row_codes"):
        accepted_here = jnp.arange(per_server, dtype=I32) < accepted[0]
        code = jnp.where(accepted_here, owner[:, 0], OWNERS) * 32768 + draft_ids
        code = jnp.broadcast_to(code.reshape(1, 1, per_server), (REPLICAS, 1, per_server))
        codes = lax.all_to_all(code, "replica", 0, 0)

    with jax.named_scope("gather_features"):
        mine = features.transpose(1, 0, 2)
        before_z = lax.ppermute(mine, "replica", Z_UP)
        after_z = lax.ppermute(mine, "replica", Z_DOWN)
        across = lax.ppermute(mine, "replica", Y_SWAP)
    mine, before_z, after_z, across, codes = together(mine, before_z, after_z, across, codes)
    pieces_first = ((mine, before_z), (after_z, across))

    with jax.named_scope("gather_features"):
        across_before = lax.ppermute(across, "replica", Z_UP)
        across_after = lax.ppermute(across, "replica", Z_DOWN)
        half = per_server // 2
        opposite = (
            lax.ppermute(before_z[:, :half], "replica", Z_UP),
            lax.ppermute(after_z[:, half:], "replica", Z_DOWN),
        )
    with jax.named_scope("unite_first"):
        give = project(pieces_first, weight, 1 - core, BF, LONG)
        given_first = swap_cores(give)
    with jax.named_scope("row_order"):
        up, down, two = (z + 3) % 4, (z + 1) % 4, (z + 2) % 4
        here, there = y_hi * 4, (1 - y_hi) * 4
        low = [here + z, here + up, there + up, there + down]
        high = [here + down, there + z, here + two, there + two]
        order = jnp.where(core == 0, jnp.stack(low + high), jnp.stack(high + low))
        order_hot = order[:, None] == jnp.arange(REPLICAS, dtype=I32)[None, :]
        place_of = jnp.sum(
            jnp.where(order_hot, jnp.arange(REPLICAS, dtype=I32)[:, None], 0), axis=0
        )

    with jax.named_scope("row_codes"):
        codes = codes.reshape(rows)
        row_owner = codes // 32768
        row_id = codes % 32768
        lane = jnp.arange(128, dtype=I32)
        picks = (row_owner[:, None] == lane[None, :]) & (lane[None, :] < OWNERS)
        earlier = jnp.arange(rows)[:, None] > jnp.arange(rows)[None, :]
        before = dot(earlier.astype(BF), picks.astype(BF))
        rank = jnp.sum(jnp.where(picks, before, 0.0), axis=1).astype(I32)
        counts = jnp.sum(picks.astype(I32), axis=0)[:OWNERS]
        placed = row_owner < OWNERS
        target = jnp.where(placed, row_owner * capacity + rank, -1)
        row_place = place_of[:, None] * per_server + jnp.arange(per_server, dtype=I32)[None, :]

    with jax.named_scope("embeds"):
        device_of = rank % OWNERS
        lanes = jnp.arange(OWNERS, dtype=I32)
        held = jnp.maximum(counts[:, None] - lanes[None, :] + OWNERS - 1, 0) // OWNERS
        base = jnp.cumsum(held, axis=0) - held
        row_base = jnp.sum(
            jnp.where(
                (row_owner[:, None, None] == lanes[None, :, None])
                & (device_of[:, None, None] == lanes[None, None, :]),
                base[None],
                0,
            ),
            axis=(1, 2),
        )
        vocab_local = embed_table.shape[0]
        local_id = row_id - tensor_index * vocab_local
        found = placed & (local_id >= 0) & (local_id < vocab_local)
        spot = jnp.where(found, device_of // 2 * SPREAD + row_base + rank // OWNERS, -1)
        side = device_of % 2
        give_spot = jnp.where(side != core, spot, -1).reshape(1, rows)
        keep_spot = jnp.where(side == core, spot, -1).reshape(1, rows)
        local_id = local_id.reshape(1, rows)
        embeds_give = take_rows(give_spot, local_id, (embed_table,), 8 * SPREAD, 448)
        swapped = swap_cores(embeds_give)
        keep_spot = together(keep_spot, embeds_give)[0]
        embeds_keep = take_rows(keep_spot, local_id, (embed_table,), 8 * SPREAD, 448)
        (summed_embeds,) = add_split(embeds_keep, swapped, 1)
        landed_embeds = to_chips(summed_embeds.reshape(8, SPREAD, cols))
    across_before, across_after, opposite, mine, _ = together(
        across_before, across_after, opposite, mine, summed_embeds
    )
    pieces_first = ((mine, before_z), (after_z, across))

    with jax.named_scope("gather_features"):
        across_opposite = (
            lax.ppermute(across_before[:, :half], "replica", Z_UP),
            lax.ppermute(across_after[:, half:], "replica", Z_DOWN),
        )
    with jax.named_scope("unite_first"):
        kept_first = project(pieces_first, weight, core, F32, LONG)
    across_opposite, kept_first = together(across_opposite, kept_first)
    pieces_second = ((across_before, across_after), opposite + across_opposite)

    with jax.named_scope("unite_second"):
        give = project(pieces_second, weight, 1 - core, BF, SHORT)
        given_second = swap_cores(give)
        kept_second = project(
            ((together(across_before, give)[0], across_after), pieces_second[1]),
            weight,
            core,
            F32,
            SHORT,
        )
        summed = add_halves((kept_first, kept_second), (given_first, given_second))
    summed, landed_embeds, across_opposite = together(summed, landed_embeds, across_opposite)
    pieces_second = ((across_before, across_after), opposite + across_opposite)

    gain_row = hidden_gain.reshape(1, cols)
    with jax.named_scope("unite"):
        parts = to_chips(summed)
    with jax.named_scope("embeds"):
        arrived = jnp.sum(landed_embeds.astype(F32), axis=0).astype(BF)
        my_held = pick(held, tensor_index, 1)
        my_base = pick(base, tensor_index, 1)
        step = jnp.arange(steps, dtype=I32)
        want = jnp.where(step[None, :] < my_held[:, None], my_base[:, None] + step[None, :], -1)
        want = want.reshape(8, 2, steps)
        want = jnp.stack([pick(want, 1 - core, 1), pick(want, core, 1)]).reshape(capacity)
        lay = want[:, None] == jnp.arange(SPREAD, dtype=I32)[None, :]
        laid = dot(lay.astype(BF), arrived).astype(BF).reshape(2, 8, steps, cols)
        swapped = swap_cores(laid[0])
        first = jnp.where(core == 0, laid[1], swapped)
        second = jnp.where(core == 0, swapped, laid[1])
        blank = jnp.zeros((8, RIDE - 2 * steps, cols), BF)
        pairs = jnp.concatenate([first, second, blank], axis=1)
    with jax.named_scope("grad_fc"):
        turned = turn(sum(pieces_first + pieces_second, ()))
    parts, pairs, turned = together(parts, pairs, turned)

    with jax.named_scope("unite"):
        own = to_chips(sum_and_spread(parts, pairs))
    with jax.named_scope("cotangent_rows"):
        cots = take_rows(
            row_place.reshape(1, rows), target.reshape(1, rows), (grads,), rows, 384
        )

    own, cots = together(own, cots)

    with jax.named_scope("unite_second"):
        united = (own, swap_cores(own))
    with jax.named_scope("norms"):
        sums = half_sums(own, cots, gain_row, per_server)
        message = partial_sums(order, sums, own, united[1], cots, gain_row, per_server)
    united, message, position = together(
        united, message, (target - tensor_index * capacity)
    )
    position = position.reshape(REPLICAS, 1, per_server)

    with jax.named_scope("norms"):
        totals = lax.all_to_all(message, "replica", 0, 0)
    with jax.named_scope("draft_input"):
        found = slot_rows(order, position, united, capacity)
    totals, found = together(totals, found)

    with jax.named_scope("grad_fc"):
        grad_fc = weight_gradient(
            order, core, turned, united, cots, gain_row, totals, model
        )
    with jax.named_scope("draft_input"):
        draft_embed, draft_hidden = normed_rows(
            position, found, own, gain_row, embed_gain.reshape(1, cols), totals, model
        )
        draft_embed = draft_embed.reshape(OWNERS, steps, cols).transpose(1, 0, 2)
        draft_embed = draft_embed.reshape(capacity, cols)
        draft_input = jnp.stack([draft_embed, draft_hidden], axis=1)
    return (draft_input, grad_fc)


def solution(mesh):
    return jax.shard_map(
        body,
        mesh=mesh,
        in_specs=(
            P("replica", None, "tensor"),
            P("replica"),
            P("replica", None),
            P("replica"),
            P(None, "tensor", "replica"),
            P("tensor", "replica"),
            P("replica"),
            P("replica"),
            P("tensor", "replica"),
        ),
        out_specs=(P("tensor", None, "replica"), P(None, "tensor", "replica")),
        check_vma=False,
    )
```

```python
import functools

import jax
import jax.numpy as jnp
from jax import lax
from jax.experimental import pallas as pl
from jax.experimental.pallas import tpu as pltpu
from jax.sharding import PartitionSpec as P

TAPS = 3
EPSILON = 1e-05
BF = jnp.bfloat16
F32 = jnp.float32
I32 = jnp.int32
SPREAD = 112
CHUNK = 48
RIDE = 32
LONG = pl.CostEstimate(flops=10**11, bytes_accessed=10**9, transcendentals=0)
SHORT = pl.CostEstimate(flops=10**6, bytes_accessed=10**5, transcendentals=0)
MIB = 1024 * 1024
OWNERS = 16
REPLICAS = 8

CHIP_GROUPS = [[2 * chip + core for chip in range(8)] for core in (0, 1)]
CORE_SWAP = [(i, i ^ 1) for i in range(16)]
Y_SWAP = [(i, i ^ 4) for i in range(8)]
Z_UP = [(i, i // 4 * 4 + (i + 1) % 4) for i in range(8)]
Z_DOWN = [(i, i // 4 * 4 + (i + 3) % 4) for i in range(8)]


def to_chips(x):
    return lax.all_to_all(x, "tensor", 0, 0, axis_index_groups=CHIP_GROUPS)


def from_replicas(x):
    spread = jnp.broadcast_to(x[None], (REPLICAS,) + x.shape)
    return lax.all_to_all(spread, "replica", 0, 0)


def swap_cores(x):
    return lax.ppermute(x, "tensor", CORE_SWAP)


def dot(a, b):
    return jnp.dot(a, b, preferred_element_type=F32)


def together(*xs):
    return lax.optimization_barrier(xs)


def pick(x, index, axis=0):
    return lax.dynamic_index_in_dim(x, index, axis, keepdims=False)


def whole(shape):
    return pl.BlockSpec(shape, lambda *_: (0,) * len(shape))


def project(sides, weight, which, out_dtype, cost):
    per_server, cols = sides[0][0].shape[1], weight.shape[1]
    first = len(sides[0])
    total = first + len(sides[1])

    def kernel(which_ref, *refs):
        w_ref, out_ref = refs[total:]

        def run(pieces):
            x = jnp.concatenate(
                [jnp.concatenate([p[t] for p in pieces], axis=0) for t in range(TAPS)], axis=1
            )
            out_ref[...] = dot(x, w_ref[...]).astype(out_ref.dtype)

        @pl.when(which_ref[0] == 0)
        def _():
            run(refs[:first])

        @pl.when(which_ref[0] != 0)
        def _():
            run(refs[first:total])

    vmem = pl.BlockSpec()
    return pl.pallas_call(
        kernel,
        out_shape=jax.ShapeDtypeStruct((2 * per_server, cols), out_dtype),
        in_specs=[pl.BlockSpec(memory_space=pltpu.SMEM)] + [vmem] * (total + 1),
        out_specs=vmem,
        compiler_params=pltpu.CompilerParams(vmem_limit_bytes=24 * 1024 * 1024),
        cost_estimate=cost,
        name="project",
    )(which.reshape(1), *sides[0], *sides[1], weight)


def sum_and_spread(parts, extra):
    chips, each, cols = parts.shape
    more = extra.shape[1]

    def kernel(parts_ref, extra_ref, out_ref):
        out_ref[:, each : each + more] = extra_ref[...]
        for first in range(0, each, 16):
            here = slice(first, first + 16)
            total = parts_ref[0, here].astype(F32)
            for k in range(1, chips):
                total = total + parts_ref[k, here].astype(F32)
            total = total.astype(BF)
            for k in range(chips):
                out_ref[k, here] = total

    vmem = pl.BlockSpec()
    return pl.pallas_call(
        kernel,
        out_shape=jax.ShapeDtypeStruct((chips, each + more, cols), BF),
        in_specs=[vmem] * 2,
        out_specs=vmem,
        compiler_params=pltpu.CompilerParams(vmem_limit_bytes=16 * MIB),
        cost_estimate=SHORT,
        name="sum_and_spread",
    )(parts, extra)


def take_rows(position, value, tables, count, step):
    length, cols = tables[0].shape
    total = position.shape[1]

    def kernel(position_ref, value_ref, *refs):
        first = pl.program_id(0) * step
        row = lax.broadcasted_iota(I32, (step, total), 0) + first
        match = row == position_ref[...]
        index = jnp.sum(jnp.where(match, value_ref[...] + 1, 0), axis=1, keepdims=True) - 1
        found = None
        for at, table_ref in enumerate(refs[:-1]):
            hot = lax.broadcasted_iota(I32, (step, length), 1) + at * length == index
            part = dot(jnp.where(hot, 1.0, 0.0).astype(BF), table_ref[...])
            found = part if found is None else found + part
        refs[-1][...] = found.astype(BF)

    return pl.pallas_call(
        kernel,
        grid=(count // step,),
        out_shape=jax.ShapeDtypeStruct((count, cols), BF),
        in_specs=[whole((1, total)), whole((1, total))] + [whole((length, cols))] * len(tables),
        out_specs=pl.BlockSpec((step, cols), lambda i: (i, 0)),
        compiler_params=pltpu.CompilerParams(vmem_limit_bytes=40 * MIB),
        cost_estimate=LONG,
        name="take_rows",
    )(position, value, *tables)


def add_halves(keeps, received):
    pair, cols = keeps[0].shape
    each = pair // 8

    def kernel(k0, r0, k1, r1, out_ref):
        for chip in range(8):
            rows = slice(chip * each, chip * each + each)
            for at, (k, r) in enumerate(((k0, r0), (k1, r1))):
                total = (k[rows] + r[rows].astype(F32)).astype(BF)
                out_ref[chip, at * each : at * each + each] = total

    vmem = pl.BlockSpec()
    return pl.pallas_call(
        kernel,
        out_shape=jax.ShapeDtypeStruct((8, 2 * each, cols), BF),
        in_specs=[vmem] * 4,
        out_specs=vmem,
        compiler_params=pltpu.CompilerParams(vmem_limit_bytes=16 * MIB),
        cost_estimate=SHORT,
        name="add_halves",
    )(keeps[0], received[0], keeps[1], received[1])


def add_split(a, b, parts):
    size = a.shape[0] // parts
    cols = a.shape[1]

    def kernel(a_ref, b_ref, *outs):
        for k, out in enumerate(outs):
            out[...] = a_ref[k * size : k * size + size] + b_ref[k * size : k * size + size]

    vmem = pl.BlockSpec()
    return pl.pallas_call(
        kernel,
        out_shape=[jax.ShapeDtypeStruct((size, cols), BF)] * parts,
        in_specs=[vmem] * 2,
        out_specs=[vmem] * parts,
        compiler_params=pltpu.CompilerParams(vmem_limit_bytes=16 * MIB),
        cost_estimate=SHORT,
        name="add_split",
    )(a, b)


def rows_at(united_refs, place):
    ref = united_refs[place // 4]
    size = CHUNK
    chunk = place % 4 // 2
    block = ref[4 * (place % 2) : 4 * (place % 2) + 4, chunk * size : chunk * size + size]
    return block.reshape(4 * size, ref.shape[2])


def landed_rows(own_ref):
    block = own_ref[:, 2 * CHUNK : 2 * CHUNK + RIDE].astype(F32)[:, :24]
    return block.reshape(8 * 24, block.shape[2])


def column_of(row, size):
    eye = lax.broadcasted_iota(I32, (size, size), 0) == lax.broadcasted_iota(I32, (size, size), 1)
    return jnp.sum(jnp.where(eye, row, 0.0), axis=1, keepdims=True)


def row_of(column, size):
    eye = lax.broadcasted_iota(I32, (size, size), 0) == lax.broadcasted_iota(I32, (size, size), 1)
    return jnp.sum(jnp.where(eye, column, 0.0), axis=0, keepdims=True)


def half_sums(rows, cots, gain, per_server):
    cols = gain.shape[1]
    side = 4 * per_server

    def kernel(rows_ref, cots_ref, gain_ref, out_ref):
        for k in range(4):
            u = rows_at((rows_ref,), k).astype(F32)
            w = cots_ref[k * per_server : k * per_server + per_server].astype(F32) * gain_ref[...]
            square = row_of(jnp.sum(u * u, axis=1, keepdims=True), per_server)
            inner = row_of(jnp.sum(u * w, axis=1, keepdims=True), per_server)
            out_ref[k] = jnp.concatenate([square, inner], axis=0)

    return pl.pallas_call(
        kernel,
        grid=(1,),
        out_shape=jax.ShapeDtypeStruct((4, 2, per_server), F32),
        in_specs=[
            whole(rows.shape),
            pl.BlockSpec((side, cols), lambda i: (0, 0)),
            whole((1, cols)),
        ],
        out_specs=whole((4, 2, per_server)),
        compiler_params=pltpu.CompilerParams(vmem_limit_bytes=24 * MIB),
        cost_estimate=SHORT,
        name="half_sums",
    )(rows, cots, gain)


def partial_sums(order, sums, own, other, cots, gain, per_server):
    cols = gain.shape[1]
    side = 4 * per_server

    def kernel(order_ref, sums_ref, own_ref, other_ref, cots_ref, gain_ref, out_ref):
        for k in range(4):
            u = rows_at((other_ref,), k).astype(F32)
            w = cots_ref[k * per_server : k * per_server + per_server].astype(F32) * gain_ref[...]
            square = row_of(jnp.sum(u * u, axis=1, keepdims=True), per_server)
            inner = row_of(jnp.sum(u * w, axis=1, keepdims=True), per_server)
            both = jnp.concatenate([square, inner], axis=0)
            for to in range(REPLICAS):
                out_ref[to, order_ref[k]] = sums_ref[k]
                out_ref[to, order_ref[k + 4]] = both
        e = landed_rows(own_ref).astype(F32)
        square = row_of(jnp.sum(e * e, axis=1, keepdims=True), per_server)
        both = jnp.concatenate([square, square], axis=0)
        for to in range(REPLICAS):
            out_ref[to, REPLICAS] = both

    shape = (REPLICAS, REPLICAS + 1, 2, per_server)
    return pl.pallas_call(
        kernel,
        grid=(1,),
        out_shape=jax.ShapeDtypeStruct(shape, F32),
        in_specs=[
            pl.BlockSpec(memory_space=pltpu.SMEM),
            whole(sums.shape),
            whole(own.shape),
            whole(other.shape),
            pl.BlockSpec((side, cols), lambda i: (1, 0)),
            whole((1, cols)),
        ],
        out_specs=whole(shape),
        compiler_params=pltpu.CompilerParams(vmem_limit_bytes=24 * MIB),
        cost_estimate=SHORT,
        name="partial_sums",
    )(order, sums, own, other, cots, gain)


def turn(pieces):
    taps, _, feat = pieces[0].shape
    rows = sum(piece.shape[1] for piece in pieces)

    def kernel(*refs):
        x = jnp.concatenate([ref[0] for ref in refs[:-1]], axis=0)
        refs[-1][0] = x.T

    return pl.pallas_call(
        kernel,
        grid=(taps,),
        out_shape=jax.ShapeDtypeStruct((taps, feat, rows), BF),
        in_specs=[pl.BlockSpec((1, p.shape[1], feat), lambda t: (t, 0, 0)) for p in pieces],
        out_specs=pl.BlockSpec((1, feat, rows), lambda t: (t, 0, 0)),
        compiler_params=pltpu.CompilerParams(vmem_limit_bytes=24 * MIB),
        cost_estimate=SHORT,
        name="turn",
    )(*pieces)


def weight_gradient(order, core, turned, united, cots, gain, totals, model):
    taps, feat, rows = turned.shape
    per_server = rows // REPLICAS
    cols = cots.shape[1]
    places = ([0, 1, 4, 5, 2, 3, 6, 7], [4, 5, 0, 1, 6, 7, 2, 3])

    def kernel(order_ref, core_ref, *refs):
        united_refs = refs[1:3]
        turned_ref, cots_ref, gain_ref, totals_ref, out_ref, g_ref = refs[:1] + refs[3:]

        @pl.when(pl.program_id(0) == 0)
        def _():
            for place in range(REPLICAS):
                both = totals_ref[0, order_ref[place]]
                for source in range(1, REPLICAS):
                    both = both + totals_ref[source, order_ref[place]]
                r = lax.rsqrt(both[0:1] / model + EPSILON)
                s = r * r * both[1:2] / model
                r = column_of(r, per_server)
                s = column_of(s, per_server)
                here = jnp.where(core_ref[0] == 0, places[0].index(place), places[1].index(place))
                size = per_server // 4
                for part in range(4):
                    at = part * size
                    chunk = place % 4 // 2 * size
                    u = united_refs[place // 4][4 * (place % 2) + part, chunk : chunk + size]
                    u = u.astype(F32)
                    w = cots_ref[place * per_server + at : place * per_server + at + size]
                    w = w.astype(F32) * gain_ref[...]
                    g = r[at : at + size] * (w - u * s[at : at + size])
                    start = pl.multiple_of(here * per_server + at, size)
                    g_ref[pl.ds(start, size)] = g.astype(BF)

        out_ref[0] = dot(turned_ref[0], g_ref[...])

    smem = pl.BlockSpec(memory_space=pltpu.SMEM)
    return pl.pallas_call(
        kernel,
        grid=(taps,),
        out_shape=jax.ShapeDtypeStruct((taps, feat, cols), F32),
        in_specs=[smem, smem]
        + [pl.BlockSpec((1, feat, rows), lambda t: (t, 0, 0))]
        + [whole(united[0].shape)] * 2
        + [whole((rows, cols)), whole((1, cols)), whole(totals.shape)],
        out_specs=pl.BlockSpec((1, feat, cols), lambda t: (t, 0, 0)),
        scratch_shapes=[pltpu.VMEM((rows, cols), BF)],
        compiler_params=pltpu.CompilerParams(vmem_limit_bytes=48 * MIB),
        cost_estimate=LONG,
        name="weight_gradient",
    )(order, core.reshape(1), turned, *united, cots, gain, totals)


def slot_rows(order, position, united, capacity):
    cols = united[0].shape[2]
    per_server = position.shape[2]

    def kernel(order_ref, position_ref, own_ref, other_ref, out_ref):
        slot = lax.broadcasted_iota(I32, (capacity, per_server), 0)
        found = jnp.zeros((capacity, cols), F32)
        for place in range(REPLICAS):
            match = slot == position_ref[order_ref[place]]
            hot = jnp.where(match, 1.0, 0.0).astype(BF)
            found = found + dot(hot, rows_at((own_ref, other_ref), place))
        out_ref[...] = found.astype(BF)

    vmem = pl.BlockSpec()
    return pl.pallas_call(
        kernel,
        out_shape=jax.ShapeDtypeStruct((capacity, cols), BF),
        in_specs=[pl.BlockSpec(memory_space=pltpu.SMEM)] + [vmem] * 3,
        out_specs=vmem,
        compiler_params=pltpu.CompilerParams(vmem_limit_bytes=24 * MIB),
        cost_estimate=SHORT,
        name="slot_rows",
    )(order, position, *united)


def normed_rows(position, found, own, gain, embed_gain, totals, model):
    capacity, cols = found.shape
    per_server = position.shape[2]

    def kernel(
        position_ref, found_ref, own_ref, gain_ref, embed_gain_ref, totals_ref, embed_ref, out_ref
    ):
        slot = lax.broadcasted_iota(I32, (capacity, per_server), 0)
        r_slot = jnp.zeros((capacity, 1), F32)
        for replica in range(REPLICAS + 1):
            square = totals_ref[0, replica]
            for source in range(1, REPLICAS):
                square = square + totals_ref[source, replica]
            r = lax.rsqrt(square[0:1] / model + EPSILON)
            if replica < REPLICAS:
                match = slot == position_ref[replica]
                r_slot = r_slot + jnp.sum(jnp.where(match, r, 0.0), axis=1, keepdims=True)
            else:
                r_embed = column_of(r, per_server)
        out_ref[...] = (found_ref[...].astype(F32) * r_slot * gain_ref[...]).astype(BF)
        embed_ref[...] = (landed_rows(own_ref) * r_embed * embed_gain_ref[...]).astype(BF)

    vmem = pl.BlockSpec()
    return pl.pallas_call(
        kernel,
        out_shape=[jax.ShapeDtypeStruct((capacity, cols), BF)] * 2,
        in_specs=[vmem] * 6,
        out_specs=[vmem] * 2,
        compiler_params=pltpu.CompilerParams(vmem_limit_bytes=16 * MIB),
        cost_estimate=SHORT,
        name="normed_rows",
    )(position, found, own, gain, embed_gain, totals)


def body(
    features,
    accepted,
    owner,
    draft_ids,
    fc_weight,
    embed_table,
    embed_gain,
    hidden_gain,
    hidden_grad,
):
    tensor_index = lax.axis_index("tensor")
    replica_index = lax.axis_index("replica")
    core = tensor_index % 2
    y_hi = replica_index // 4
    z = replica_index % 4
    per_server = features.shape[0]
    capacity = hidden_grad.shape[0]
    steps = capacity // OWNERS
    feat = features.shape[2]
    width = TAPS * feat
    cols = fc_weight.shape[2]
    model = cols * REPLICAS
    rows = per_server * REPLICAS
    pair = 2 * per_server

    weight = fc_weight.reshape(width, cols)

    with jax.named_scope("gather_cotangents"):
        grads = lax.all_gather(hidden_grad, "tensor", axis=0, tiled=True)

    with jax.named_scope("row_codes"):
        accepted_here = jnp.arange(per_server, dtype=I32) < accepted[0]
        code = jnp.where(accepted_here, owner[:, 0], OWNERS) * 32768 + draft_ids
        code = jnp.broadcast_to(code.reshape(1, 1, per_server), (REPLICAS, 1, per_server))
        codes = lax.all_to_all(code, "replica", 0, 0)

    with jax.named_scope("gather_features"):
        mine = features.transpose(1, 0, 2)
        before_z = lax.ppermute(mine, "replica", Z_UP)
        after_z = lax.ppermute(mine, "replica", Z_DOWN)
        across = lax.ppermute(mine, "replica", Y_SWAP)
    mine, before_z, after_z, across, codes = together(mine, before_z, after_z, across, codes)
    pieces_first = ((mine, before_z), (after_z, across))

    with jax.named_scope("gather_features"):
        across_before = lax.ppermute(across, "replica", Z_UP)
        across_after = lax.ppermute(across, "replica", Z_DOWN)
        opposite = lax.ppermute(before_z, "replica", Z_UP)
    with jax.named_scope("row_order"):
        up, down, two = (z + 3) % 4, (z + 1) % 4, (z + 2) % 4
        here, there = y_hi * 4, (1 - y_hi) * 4
        low = [here + z, here + up, there + up, there + down]
        high = [here + down, there + z, here + two, there + two]
        order = jnp.where(core == 0, jnp.stack(low + high), jnp.stack(high + low))
        order_hot = order[:, None] == jnp.arange(REPLICAS, dtype=I32)[None, :]
        place_of = jnp.sum(
            jnp.where(order_hot, jnp.arange(REPLICAS, dtype=I32)[:, None], 0), axis=0
        )

    with jax.named_scope("row_codes"):
        codes = codes.reshape(rows)
        row_owner = codes // 32768
        row_id = codes % 32768
        lane = jnp.arange(128, dtype=I32)
        picks = (row_owner[:, None] == lane[None, :]) & (lane[None, :] < OWNERS)
        earlier = jnp.arange(rows)[:, None] > jnp.arange(rows)[None, :]
        before = dot(earlier.astype(BF), picks.astype(BF))
        rank = jnp.sum(jnp.where(picks, before, 0.0), axis=1).astype(I32)
        counts = jnp.sum(picks.astype(I32), axis=0)[:OWNERS]
        placed = row_owner < OWNERS
        target = jnp.where(placed, row_owner * capacity + rank, -1)
        row_place = place_of[:, None] * per_server + jnp.arange(per_server, dtype=I32)[None, :]

    with jax.named_scope("embeds"):
        device_of = rank % OWNERS
        lanes = jnp.arange(OWNERS, dtype=I32)
        held = jnp.maximum(counts[:, None] - lanes[None, :] + OWNERS - 1, 0) // OWNERS
        base = jnp.cumsum(held, axis=0) - held
        row_base = jnp.sum(
            jnp.where(
                (row_owner[:, None, None] == lanes[None, :, None])
                & (device_of[:, None, None] == lanes[None, None, :]),
                base[None],
                0,
            ),
            axis=(1, 2),
        )
        vocab_local = embed_table.shape[0]
        local_id = row_id - tensor_index * vocab_local
        found = placed & (local_id >= 0) & (local_id < vocab_local)
        spot = jnp.where(found, device_of // 2 * SPREAD + row_base + rank // OWNERS, -1)
        side = device_of % 2
        give_spot = jnp.where(side != core, spot, -1).reshape(1, rows)
        keep_spot = jnp.where(side == core, spot, -1).reshape(1, rows)
        local_id = local_id.reshape(1, rows)
        embeds_give = take_rows(give_spot, local_id, (embed_table,), 8 * SPREAD, 448)
        swapped = swap_cores(embeds_give)
        keep_spot = together(keep_spot, embeds_give)[0]
        embeds_keep = take_rows(keep_spot, local_id, (embed_table,), 8 * SPREAD, 448)
        (summed_embeds,) = add_split(embeds_keep, swapped, 1)
        landed_embeds = to_chips(summed_embeds.reshape(8, SPREAD, cols))
    across_before, across_after, mine, _ = together(
        across_before, across_after, mine, summed_embeds
    )
    pieces_first = ((mine, before_z), (after_z, across))

    with jax.named_scope("gather_features"):
        across_opposite = lax.ppermute(across_after, "replica", Z_DOWN)
    with jax.named_scope("unite_first"):
        give = project(pieces_first, weight, 1 - core, BF, LONG)
        given_first = swap_cores(give)
        kept_first = project(pieces_first, weight, core, F32, LONG)
    across_opposite, opposite, kept_first = together(across_opposite, opposite, kept_first)
    pieces_second = ((across_before, across_after), (opposite, across_opposite))

    with jax.named_scope("unite_second"):
        give = project(pieces_second, weight, 1 - core, BF, SHORT)
        given_second = swap_cores(give)
        kept_second = project(
            ((together(across_before, give)[0], across_after), pieces_second[1]),
            weight,
            core,
            F32,
            SHORT,
        )
        summed = add_halves((kept_first, kept_second), (given_first, given_second))
    summed, landed_embeds, across_opposite = together(summed, landed_embeds, across_opposite)
    pieces_second = ((across_before, across_after), (opposite, across_opposite))

    gain_row = hidden_gain.reshape(1, cols)
    with jax.named_scope("unite"):
        parts = to_chips(summed)
    with jax.named_scope("embeds"):
        arrived = jnp.sum(landed_embeds.astype(F32), axis=0).astype(BF)
        my_held = pick(held, tensor_index, 1)
        my_base = pick(base, tensor_index, 1)
        step = jnp.arange(steps, dtype=I32)
        want = jnp.where(step[None, :] < my_held[:, None], my_base[:, None] + step[None, :], -1)
        want = want.reshape(8, 2, steps)
        want = jnp.stack([pick(want, 1 - core, 1), pick(want, core, 1)]).reshape(capacity)
        lay = want[:, None] == jnp.arange(SPREAD, dtype=I32)[None, :]
        laid = dot(lay.astype(BF), arrived).astype(BF).reshape(2, 8, steps, cols)
        swapped = swap_cores(laid[0])
        first = jnp.where(core == 0, laid[1], swapped)
        second = jnp.where(core == 0, swapped, laid[1])
        blank = jnp.zeros((8, RIDE - 2 * steps, cols), BF)
        pairs = jnp.concatenate([first, second, blank], axis=1)
    with jax.named_scope("grad_fc"):
        turned = turn(sum(pieces_first + pieces_second, ()))
    parts, pairs, turned = together(parts, pairs, turned)

    with jax.named_scope("unite"):
        own = to_chips(sum_and_spread(parts, pairs))
    with jax.named_scope("cotangent_rows"):
        cots = take_rows(
            row_place.reshape(1, rows), target.reshape(1, rows), (grads,), rows, 384
        )

    own, cots = together(own, cots)

    with jax.named_scope("unite_second"):
        united = (own, swap_cores(own))
    with jax.named_scope("norms"):
        sums = half_sums(own, cots, gain_row, per_server)
        message = partial_sums(order, sums, own, united[1], cots, gain_row, per_server)
    united, message, position = together(
        united, message, (target - tensor_index * capacity)
    )
    position = position.reshape(REPLICAS, 1, per_server)

    with jax.named_scope("norms"):
        totals = lax.all_to_all(message, "replica", 0, 0)
    with jax.named_scope("draft_input"):
        found = slot_rows(order, position, united, capacity)
    totals, found = together(totals, found)

    with jax.named_scope("grad_fc"):
        grad_fc = weight_gradient(
            order, core, turned, united, cots, gain_row, totals, model
        )
    with jax.named_scope("draft_input"):
        draft_embed, draft_hidden = normed_rows(
            position, found, own, gain_row, embed_gain.reshape(1, cols), totals, model
        )
        draft_embed = draft_embed.reshape(OWNERS, steps, cols).transpose(1, 0, 2)
        draft_embed = draft_embed.reshape(capacity, cols)
        draft_input = jnp.stack([draft_embed, draft_hidden], axis=1)
    return (draft_input, grad_fc)


def solution(mesh):
    return jax.shard_map(
        body,
        mesh=mesh,
        in_specs=(
            P("replica", None, "tensor"),
            P("replica"),
            P("replica", None),
            P("replica"),
            P(None, "tensor", "replica"),
            P("tensor", "replica"),
            P("replica"),
            P("replica"),
            P("tensor", "replica"),
        ),
        out_specs=(P("tensor", None, "replica"), P(None, "tensor", "replica")),
        check_vma=False,
    )
```

```python
import functools

import jax
import jax.numpy as jnp
from jax import lax
from jax.experimental import pallas as pl
from jax.experimental.pallas import tpu as pltpu
from jax.sharding import PartitionSpec as P

TAPS = 3
EPSILON = 1e-05
BF = jnp.bfloat16
F32 = jnp.float32
I32 = jnp.int32
SPREAD = 112
CHUNK = 48
RIDE = 32
LONG = pl.CostEstimate(flops=10**11, bytes_accessed=10**9, transcendentals=0)
SHORT = pl.CostEstimate(flops=10**6, bytes_accessed=10**5, transcendentals=0)
MIB = 1024 * 1024
OWNERS = 16
REPLICAS = 8

CHIP_GROUPS = [[2 * chip + core for chip in range(8)] for core in (0, 1)]
CORE_SWAP = [(i, i ^ 1) for i in range(16)]
Y_SWAP = [(i, i ^ 4) for i in range(8)]
Z_UP = [(i, i // 4 * 4 + (i + 1) % 4) for i in range(8)]
Z_DOWN = [(i, i // 4 * 4 + (i + 3) % 4) for i in range(8)]


def to_chips(x):
    return lax.all_to_all(x, "tensor", 0, 0, axis_index_groups=CHIP_GROUPS)


def from_replicas(x):
    spread = jnp.broadcast_to(x[None], (REPLICAS,) + x.shape)
    return lax.all_to_all(spread, "replica", 0, 0)


def swap_cores(x):
    return lax.ppermute(x, "tensor", CORE_SWAP)


def dot(a, b):
    return jnp.dot(a, b, preferred_element_type=F32)


def together(*xs):
    return lax.optimization_barrier(xs)


def pick(x, index, axis=0):
    return lax.dynamic_index_in_dim(x, index, axis, keepdims=False)


def whole(shape):
    return pl.BlockSpec(shape, lambda *_: (0,) * len(shape))


def project(sides, weight, which, out_dtype, cost):
    per_server, cols = sides[0][0].shape[1], weight.shape[1]
    first = len(sides[0])
    total = first + len(sides[1])

    def kernel(which_ref, *refs):
        w_ref, out_ref = refs[total:]

        def run(pieces):
            x = jnp.concatenate(
                [jnp.concatenate([p[t] for p in pieces], axis=0) for t in range(TAPS)], axis=1
            )
            out_ref[...] = dot(x, w_ref[...]).astype(out_ref.dtype)

        @pl.when(which_ref[0] == 0)
        def _():
            run(refs[:first])

        @pl.when(which_ref[0] != 0)
        def _():
            run(refs[first:total])

    vmem = pl.BlockSpec()
    return pl.pallas_call(
        kernel,
        out_shape=jax.ShapeDtypeStruct((2 * per_server, cols), out_dtype),
        in_specs=[pl.BlockSpec(memory_space=pltpu.SMEM)] + [vmem] * (total + 1),
        out_specs=vmem,
        compiler_params=pltpu.CompilerParams(vmem_limit_bytes=24 * 1024 * 1024),
        cost_estimate=cost,
        name="project",
    )(which.reshape(1), *sides[0], *sides[1], weight)


def sum_and_spread(parts, extra):
    chips, each, cols = parts.shape
    more = extra.shape[1]

    def kernel(parts_ref, extra_ref, out_ref):
        out_ref[:, each : each + more] = extra_ref[...]
        for first in range(0, each, 16):
            here = slice(first, first + 16)
            total = parts_ref[0, here].astype(F32)
            for k in range(1, chips):
                total = total + parts_ref[k, here].astype(F32)
            total = total.astype(BF)
            for k in range(chips):
                out_ref[k, here] = total

    vmem = pl.BlockSpec()
    return pl.pallas_call(
        kernel,
        out_shape=jax.ShapeDtypeStruct((chips, each + more, cols), BF),
        in_specs=[vmem] * 2,
        out_specs=vmem,
        compiler_params=pltpu.CompilerParams(vmem_limit_bytes=16 * MIB),
        cost_estimate=SHORT,
        name="sum_and_spread",
    )(parts, extra)


def take_rows(position, value, tables, count, step):
    length, cols = tables[0].shape
    total = position.shape[1]

    def kernel(position_ref, value_ref, *refs):
        first = pl.program_id(0) * step
        row = lax.broadcasted_iota(I32, (step, total), 0) + first
        match = row == position_ref[...]
        index = jnp.sum(jnp.where(match, value_ref[...] + 1, 0), axis=1, keepdims=True) - 1
        found = None
        for at, table_ref in enumerate(refs[:-1]):
            hot = lax.broadcasted_iota(I32, (step, length), 1) + at * length == index
            part = dot(jnp.where(hot, 1.0, 0.0).astype(BF), table_ref[...])
            found = part if found is None else found + part
        refs[-1][...] = found.astype(BF)

    return pl.pallas_call(
        kernel,
        grid=(count // step,),
        out_shape=jax.ShapeDtypeStruct((count, cols), BF),
        in_specs=[whole((1, total)), whole((1, total))] + [whole((length, cols))] * len(tables),
        out_specs=pl.BlockSpec((step, cols), lambda i: (i, 0)),
        compiler_params=pltpu.CompilerParams(vmem_limit_bytes=40 * MIB),
        cost_estimate=LONG,
        name="take_rows",
    )(position, value, *tables)


def add_halves(keeps, received):
    pair, cols = keeps[0].shape
    each = pair // 8

    def kernel(k0, r0, k1, r1, out_ref):
        for chip in range(8):
            rows = slice(chip * each, chip * each + each)
            for at, (k, r) in enumerate(((k0, r0), (k1, r1))):
                total = (k[rows] + r[rows].astype(F32)).astype(BF)
                out_ref[chip, at * each : at * each + each] = total

    vmem = pl.BlockSpec()
    return pl.pallas_call(
        kernel,
        out_shape=jax.ShapeDtypeStruct((8, 2 * each, cols), BF),
        in_specs=[vmem] * 4,
        out_specs=vmem,
        compiler_params=pltpu.CompilerParams(vmem_limit_bytes=16 * MIB),
        cost_estimate=SHORT,
        name="add_halves",
    )(keeps[0], received[0], keeps[1], received[1])


def add_split(a, b, parts):
    size = a.shape[0] // parts
    cols = a.shape[1]

    def kernel(a_ref, b_ref, *outs):
        for k, out in enumerate(outs):
            out[...] = a_ref[k * size : k * size + size] + b_ref[k * size : k * size + size]

    vmem = pl.BlockSpec()
    return pl.pallas_call(
        kernel,
        out_shape=[jax.ShapeDtypeStruct((size, cols), BF)] * parts,
        in_specs=[vmem] * 2,
        out_specs=[vmem] * parts,
        compiler_params=pltpu.CompilerParams(vmem_limit_bytes=16 * MIB),
        cost_estimate=SHORT,
        name="add_split",
    )(a, b)


def rows_at(united_refs, place):
    ref = united_refs[place // 4]
    size = CHUNK
    chunk = place % 4 // 2
    block = ref[4 * (place % 2) : 4 * (place % 2) + 4, chunk * size : chunk * size + size]
    return block.reshape(4 * size, ref.shape[2])


def landed_rows(own_ref):
    block = own_ref[:, 2 * CHUNK : 2 * CHUNK + RIDE].astype(F32)[:, :24]
    return block.reshape(8 * 24, block.shape[2])


def column_of(row, size):
    eye = lax.broadcasted_iota(I32, (size, size), 0) == lax.broadcasted_iota(I32, (size, size), 1)
    return jnp.sum(jnp.where(eye, row, 0.0), axis=1, keepdims=True)


def row_of(column, size):
    eye = lax.broadcasted_iota(I32, (size, size), 0) == lax.broadcasted_iota(I32, (size, size), 1)
    return jnp.sum(jnp.where(eye, column, 0.0), axis=0, keepdims=True)


def half_sums(rows, cots, gain, per_server):
    cols = gain.shape[1]
    side = 4 * per_server

    def kernel(rows_ref, cots_ref, gain_ref, out_ref):
        for k in range(4):
            u = rows_at((rows_ref,), k).astype(F32)
            w = cots_ref[k * per_server : k * per_server + per_server].astype(F32) * gain_ref[...]
            square = row_of(jnp.sum(u * u, axis=1, keepdims=True), per_server)
            inner = row_of(jnp.sum(u * w, axis=1, keepdims=True), per_server)
            out_ref[k] = jnp.concatenate([square, inner], axis=0)

    return pl.pallas_call(
        kernel,
        grid=(1,),
        out_shape=jax.ShapeDtypeStruct((4, 2, per_server), F32),
        in_specs=[
            whole(rows.shape),
            pl.BlockSpec((side, cols), lambda i: (0, 0)),
            whole((1, cols)),
        ],
        out_specs=whole((4, 2, per_server)),
        compiler_params=pltpu.CompilerParams(vmem_limit_bytes=24 * MIB),
        cost_estimate=SHORT,
        name="half_sums",
    )(rows, cots, gain)


def partial_sums(order, sums, own, other, cots, gain, per_server):
    cols = gain.shape[1]
    side = 4 * per_server

    def kernel(order_ref, sums_ref, own_ref, other_ref, cots_ref, gain_ref, out_ref):
        for k in range(4):
            u = rows_at((other_ref,), k).astype(F32)
            w = cots_ref[k * per_server : k * per_server + per_server].astype(F32) * gain_ref[...]
            square = row_of(jnp.sum(u * u, axis=1, keepdims=True), per_server)
            inner = row_of(jnp.sum(u * w, axis=1, keepdims=True), per_server)
            both = jnp.concatenate([square, inner], axis=0)
            for to in range(REPLICAS):
                out_ref[to, order_ref[k]] = sums_ref[k]
                out_ref[to, order_ref[k + 4]] = both
        e = landed_rows(own_ref).astype(F32)
        square = row_of(jnp.sum(e * e, axis=1, keepdims=True), per_server)
        both = jnp.concatenate([square, square], axis=0)
        for to in range(REPLICAS):
            out_ref[to, REPLICAS] = both

    shape = (REPLICAS, REPLICAS + 1, 2, per_server)
    return pl.pallas_call(
        kernel,
        grid=(1,),
        out_shape=jax.ShapeDtypeStruct(shape, F32),
        in_specs=[
            pl.BlockSpec(memory_space=pltpu.SMEM),
            whole(sums.shape),
            whole(own.shape),
            whole(other.shape),
            pl.BlockSpec((side, cols), lambda i: (1, 0)),
            whole((1, cols)),
        ],
        out_specs=whole(shape),
        compiler_params=pltpu.CompilerParams(vmem_limit_bytes=24 * MIB),
        cost_estimate=SHORT,
        name="partial_sums",
    )(order, sums, own, other, cots, gain)


def turn(pieces):
    taps, _, feat = pieces[0].shape
    rows = sum(piece.shape[1] for piece in pieces)

    def kernel(*refs):
        x = jnp.concatenate([ref[0] for ref in refs[:-1]], axis=0)
        refs[-1][0] = x.T

    return pl.pallas_call(
        kernel,
        grid=(taps,),
        out_shape=jax.ShapeDtypeStruct((taps, feat, rows), BF),
        in_specs=[pl.BlockSpec((1, p.shape[1], feat), lambda t: (t, 0, 0)) for p in pieces],
        out_specs=pl.BlockSpec((1, feat, rows), lambda t: (t, 0, 0)),
        compiler_params=pltpu.CompilerParams(vmem_limit_bytes=24 * MIB),
        cost_estimate=SHORT,
        name="turn",
    )(*pieces)


def weight_gradient(order, core, turned, united, cots, gain, totals, model):
    taps, feat, rows = turned.shape
    per_server = rows // REPLICAS
    cols = cots.shape[1]
    places = ([0, 1, 4, 5, 2, 3, 6, 7], [4, 5, 0, 1, 6, 7, 2, 3])

    def kernel(order_ref, core_ref, *refs):
        united_refs = refs[1:3]
        turned_ref, cots_ref, gain_ref, totals_ref, out_ref, g_ref = refs[:1] + refs[3:]

        @pl.when((pl.program_id(0) == 0) & (pl.program_id(1) == 0))
        def _():
            for place in range(REPLICAS):
                both = totals_ref[0, order_ref[place]]
                for source in range(1, REPLICAS):
                    both = both + totals_ref[source, order_ref[place]]
                r = lax.rsqrt(both[0:1] / model + EPSILON)
                s = r * r * both[1:2] / model
                r = column_of(r, per_server)
                s = column_of(s, per_server)
                here = jnp.where(core_ref[0] == 0, places[0].index(place), places[1].index(place))
                size = per_server // 4
                for part in range(4):
                    at = part * size
                    chunk = place % 4 // 2 * size
                    u = united_refs[place // 4][4 * (place % 2) + part, chunk : chunk + size]
                    u = u.astype(F32)
                    w = cots_ref[place * per_server + at : place * per_server + at + size]
                    w = w.astype(F32) * gain_ref[...]
                    g = r[at : at + size] * (w - u * s[at : at + size])
                    start = pl.multiple_of(here * per_server + at, size)
                    g_ref[pl.ds(start, size)] = g.astype(BF)

        out_ref[0] = dot(turned_ref[0], g_ref[...])

    smem = pl.BlockSpec(memory_space=pltpu.SMEM)
    return pl.pallas_call(
        kernel,
        grid=(taps, 2),
        out_shape=jax.ShapeDtypeStruct((taps, feat, cols), F32),
        in_specs=[smem, smem]
        + [pl.BlockSpec((1, feat // 2, rows), lambda t, h: (t, h, 0))]
        + [whole(united[0].shape)] * 2
        + [whole((rows, cols)), whole((1, cols)), whole(totals.shape)],
        out_specs=pl.BlockSpec((1, feat // 2, cols), lambda t, h: (t, h, 0)),
        scratch_shapes=[pltpu.VMEM((rows, cols), BF)],
        compiler_params=pltpu.CompilerParams(vmem_limit_bytes=48 * MIB),
        cost_estimate=LONG,
        name="weight_gradient",
    )(order, core.reshape(1), turned, *united, cots, gain, totals)


def slot_rows(order, position, united, capacity):
    cols = united[0].shape[2]
    per_server = position.shape[2]

    def kernel(order_ref, position_ref, own_ref, other_ref, out_ref):
        slot = lax.broadcasted_iota(I32, (capacity, per_server), 0)
        found = jnp.zeros((capacity, cols), F32)
        for place in range(REPLICAS):
            match = slot == position_ref[order_ref[place]]
            hot = jnp.where(match, 1.0, 0.0).astype(BF)
            found = found + dot(hot, rows_at((own_ref, other_ref), place))
        out_ref[...] = found.astype(BF)

    vmem = pl.BlockSpec()
    return pl.pallas_call(
        kernel,
        out_shape=jax.ShapeDtypeStruct((capacity, cols), BF),
        in_specs=[pl.BlockSpec(memory_space=pltpu.SMEM)] + [vmem] * 3,
        out_specs=vmem,
        compiler_params=pltpu.CompilerParams(vmem_limit_bytes=24 * MIB),
        cost_estimate=SHORT,
        name="slot_rows",
    )(order, position, *united)


def normed_rows(position, found, own, gain, embed_gain, totals, model):
    capacity, cols = found.shape
    per_server = position.shape[2]

    def kernel(
        position_ref, found_ref, own_ref, gain_ref, embed_gain_ref, totals_ref, embed_ref, out_ref
    ):
        slot = lax.broadcasted_iota(I32, (capacity, per_server), 0)
        r_slot = jnp.zeros((capacity, 1), F32)
        for replica in range(REPLICAS + 1):
            square = totals_ref[0, replica]
            for source in range(1, REPLICAS):
                square = square + totals_ref[source, replica]
            r = lax.rsqrt(square[0:1] / model + EPSILON)
            if replica < REPLICAS:
                match = slot == position_ref[replica]
                r_slot = r_slot + jnp.sum(jnp.where(match, r, 0.0), axis=1, keepdims=True)
            else:
                r_embed = column_of(r, per_server)
        out_ref[...] = (found_ref[...].astype(F32) * r_slot * gain_ref[...]).astype(BF)
        embed_ref[...] = (landed_rows(own_ref) * r_embed * embed_gain_ref[...]).astype(BF)

    vmem = pl.BlockSpec()
    return pl.pallas_call(
        kernel,
        out_shape=[jax.ShapeDtypeStruct((capacity, cols), BF)] * 2,
        in_specs=[vmem] * 6,
        out_specs=[vmem] * 2,
        compiler_params=pltpu.CompilerParams(vmem_limit_bytes=16 * MIB),
        cost_estimate=SHORT,
        name="normed_rows",
    )(position, found, own, gain, embed_gain, totals)


def body(
    features,
    accepted,
    owner,
    draft_ids,
    fc_weight,
    embed_table,
    embed_gain,
    hidden_gain,
    hidden_grad,
):
    tensor_index = lax.axis_index("tensor")
    replica_index = lax.axis_index("replica")
    core = tensor_index % 2
    y_hi = replica_index // 4
    z = replica_index % 4
    per_server = features.shape[0]
    capacity = hidden_grad.shape[0]
    steps = capacity // OWNERS
    feat = features.shape[2]
    width = TAPS * feat
    cols = fc_weight.shape[2]
    model = cols * REPLICAS
    rows = per_server * REPLICAS
    pair = 2 * per_server

    weight = fc_weight.reshape(width, cols)

    with jax.named_scope("gather_cotangents"):
        grads = lax.all_gather(hidden_grad, "tensor", axis=0, tiled=True)

    with jax.named_scope("row_codes"):
        accepted_here = jnp.arange(per_server, dtype=I32) < accepted[0]
        code = jnp.where(accepted_here, owner[:, 0], OWNERS) * 32768 + draft_ids
        code = jnp.broadcast_to(code.reshape(1, 1, per_server), (REPLICAS, 1, per_server))
        codes = lax.all_to_all(code, "replica", 0, 0)

    with jax.named_scope("gather_features"):
        mine = features.transpose(1, 0, 2)
        before_z = lax.ppermute(mine, "replica", Z_UP)
        after_z = lax.ppermute(mine, "replica", Z_DOWN)
        across = lax.ppermute(mine, "replica", Y_SWAP)
    mine, before_z, after_z, across, codes = together(mine, before_z, after_z, across, codes)
    pieces_first = ((mine, before_z), (after_z, across))

    with jax.named_scope("gather_features"):
        across_before = lax.ppermute(across, "replica", Z_UP)
        across_after = lax.ppermute(across, "replica", Z_DOWN)
        opposite = lax.ppermute(before_z, "replica", Z_UP)
    with jax.named_scope("row_order"):
        up, down, two = (z + 3) % 4, (z + 1) % 4, (z + 2) % 4
        here, there = y_hi * 4, (1 - y_hi) * 4
        low = [here + z, here + up, there + up, there + down]
        high = [here + down, there + z, here + two, there + two]
        order = jnp.where(core == 0, jnp.stack(low + high), jnp.stack(high + low))
        order_hot = order[:, None] == jnp.arange(REPLICAS, dtype=I32)[None, :]
        place_of = jnp.sum(
            jnp.where(order_hot, jnp.arange(REPLICAS, dtype=I32)[:, None], 0), axis=0
        )

    with jax.named_scope("row_codes"):
        codes = codes.reshape(rows)
        row_owner = codes // 32768
        row_id = codes % 32768
        lane = jnp.arange(128, dtype=I32)
        picks = (row_owner[:, None] == lane[None, :]) & (lane[None, :] < OWNERS)
        earlier = jnp.arange(rows)[:, None] > jnp.arange(rows)[None, :]
        before = dot(earlier.astype(BF), picks.astype(BF))
        rank = jnp.sum(jnp.where(picks, before, 0.0), axis=1).astype(I32)
        counts = jnp.sum(picks.astype(I32), axis=0)[:OWNERS]
        placed = row_owner < OWNERS
        target = jnp.where(placed, row_owner * capacity + rank, -1)
        row_place = place_of[:, None] * per_server + jnp.arange(per_server, dtype=I32)[None, :]

    with jax.named_scope("embeds"):
        device_of = rank % OWNERS
        lanes = jnp.arange(OWNERS, dtype=I32)
        held = jnp.maximum(counts[:, None] - lanes[None, :] + OWNERS - 1, 0) // OWNERS
        base = jnp.cumsum(held, axis=0) - held
        row_base = jnp.sum(
            jnp.where(
                (row_owner[:, None, None] == lanes[None, :, None])
                & (device_of[:, None, None] == lanes[None, None, :]),
                base[None],
                0,
            ),
            axis=(1, 2),
        )
        vocab_local = embed_table.shape[0]
        local_id = row_id - tensor_index * vocab_local
        found = placed & (local_id >= 0) & (local_id < vocab_local)
        spot = jnp.where(found, device_of // 2 * SPREAD + row_base + rank // OWNERS, -1)
        side = device_of % 2
        give_spot = jnp.where(side != core, spot, -1).reshape(1, rows)
        keep_spot = jnp.where(side == core, spot, -1).reshape(1, rows)
        local_id = local_id.reshape(1, rows)
        embeds_give = take_rows(give_spot, local_id, (embed_table,), 8 * SPREAD, 448)
        swapped = swap_cores(embeds_give)
        keep_spot = together(keep_spot, embeds_give)[0]
        embeds_keep = take_rows(keep_spot, local_id, (embed_table,), 8 * SPREAD, 448)
        (summed_embeds,) = add_split(embeds_keep, swapped, 1)
        landed_embeds = to_chips(summed_embeds.reshape(8, SPREAD, cols))
    across_before, across_after, mine, _ = together(
        across_before, across_after, mine, summed_embeds
    )
    pieces_first = ((mine, before_z), (after_z, across))

    with jax.named_scope("gather_features"):
        across_opposite = lax.ppermute(across_after, "replica", Z_DOWN)
    with jax.named_scope("unite_first"):
        give = project(pieces_first, weight, 1 - core, BF, LONG)
        given_first = swap_cores(give)
        kept_first = project(pieces_first, weight, core, F32, LONG)
    across_opposite, opposite, kept_first = together(across_opposite, opposite, kept_first)
    pieces_second = ((across_before, across_after), (opposite, across_opposite))

    with jax.named_scope("unite_second"):
        give = project(pieces_second, weight, 1 - core, BF, SHORT)
        given_second = swap_cores(give)
        kept_second = project(
            ((together(across_before, give)[0], across_after), pieces_second[1]),
            weight,
            core,
            F32,
            SHORT,
        )
        summed = add_halves((kept_first, kept_second), (given_first, given_second))
    summed, landed_embeds, across_opposite = together(summed, landed_embeds, across_opposite)
    pieces_second = ((across_before, across_after), (opposite, across_opposite))

    gain_row = hidden_gain.reshape(1, cols)
    with jax.named_scope("unite"):
        parts = to_chips(summed)
    with jax.named_scope("embeds"):
        arrived = jnp.sum(landed_embeds.astype(F32), axis=0).astype(BF)
        my_held = pick(held, tensor_index, 1)
        my_base = pick(base, tensor_index, 1)
        step = jnp.arange(steps, dtype=I32)
        want = jnp.where(step[None, :] < my_held[:, None], my_base[:, None] + step[None, :], -1)
        want = want.reshape(8, 2, steps)
        want = jnp.stack([pick(want, 1 - core, 1), pick(want, core, 1)]).reshape(capacity)
        lay = want[:, None] == jnp.arange(SPREAD, dtype=I32)[None, :]
        laid = dot(lay.astype(BF), arrived).astype(BF).reshape(2, 8, steps, cols)
        swapped = swap_cores(laid[0])
        first = jnp.where(core == 0, laid[1], swapped)
        second = jnp.where(core == 0, swapped, laid[1])
        blank = jnp.zeros((8, RIDE - 2 * steps, cols), BF)
        pairs = jnp.concatenate([first, second, blank], axis=1)
    with jax.named_scope("grad_fc"):
        turned = turn(sum(pieces_first + pieces_second, ()))
    parts, pairs, turned = together(parts, pairs, turned)

    with jax.named_scope("unite"):
        own = to_chips(sum_and_spread(parts, pairs))
    with jax.named_scope("cotangent_rows"):
        cots = take_rows(
            row_place.reshape(1, rows), target.reshape(1, rows), (grads,), rows, 384
        )

    own, cots = together(own, cots)

    with jax.named_scope("unite_second"):
        united = (own, swap_cores(own))
    with jax.named_scope("norms"):
        sums = half_sums(own, cots, gain_row, per_server)
        message = partial_sums(order, sums, own, united[1], cots, gain_row, per_server)
    united, message, position = together(
        united, message, (target - tensor_index * capacity)
    )
    position = position.reshape(REPLICAS, 1, per_server)

    with jax.named_scope("norms"):
        totals = lax.all_to_all(message, "replica", 0, 0)
    with jax.named_scope("draft_input"):
        found = slot_rows(order, position, united, capacity)
    totals, found = together(totals, found)

    with jax.named_scope("grad_fc"):
        grad_fc = weight_gradient(
            order, core, turned, united, cots, gain_row, totals, model
        )
    with jax.named_scope("draft_input"):
        draft_embed, draft_hidden = normed_rows(
            position, found, own, gain_row, embed_gain.reshape(1, cols), totals, model
        )
        draft_embed = draft_embed.reshape(OWNERS, steps, cols).transpose(1, 0, 2)
        draft_embed = draft_embed.reshape(capacity, cols)
        draft_input = jnp.stack([draft_embed, draft_hidden], axis=1)
    return (draft_input, grad_fc)


def solution(mesh):
    return jax.shard_map(
        body,
        mesh=mesh,
        in_specs=(
            P("replica", None, "tensor"),
            P("replica"),
            P("replica", None),
            P("replica"),
            P(None, "tensor", "replica"),
            P("tensor", "replica"),
            P("replica"),
            P("replica"),
            P("tensor", "replica"),
        ),
        out_specs=(P("tensor", None, "replica"), P(None, "tensor", "replica")),
        check_vma=False,
    )
```
